256 devices in a mesh: dp: 16 (over z, core), tensor: 16 (over y, x).
Axes of the slice: x: 4, y: 4, z: 8, core: 2. Of those that a mesh axis runs over, the one named last changes fastest.
Arguments:
- grads: bfloat16 [16, 8192, 2048], P('dp', None, 'tensor'), may hold values from -200 to 200, as said below
- error: float32 [16, 8192, 2048], P('dp', None, 'tensor'), may hold values from -4 to 4
- q_prev: float32 [2048, 32], P('tensor'), may hold values from -5 to 5
Outputs:
- synced: bfloat16 [8192, 2048], P('dp', 'tensor')
- error_out: float32 [16, 8192, 2048], P('dp', None, 'tensor')
- q_new: float32 [2048, 32], P('tensor')
The draws below stay inside these ranges and needn't reach their ends.
Inputs may be any that keep to these rules, and one draw needn't show every extreme that they name: `grads`: each replica's gradient is finite.
All inputs are finite; a program needn't handle non-finite values.
Results may differ from the reference program's by a relative error of at most 0.001.
Values sent between devices are 32-bit elements; how exact they have to be, the bound alone decides.
A program may use at most 64 MiB of HBM per device.

```python
import jax
import jax.numpy as jnp
from jax import lax

D = 8192
KVW = 2048
RANK = 32
REPLICAS = 16
N_DP = 16


def draw_grads(key, part):
    key = jax.random.fold_in(key, 11)
    key_common, key_own, key_cols = jax.random.split(key, 3)
    col_scale = jnp.exp(jax.random.uniform(key_cols, (1, KVW), jnp.float32, 0.0, 1.386))
    common = 3.0 * jnp.clip(jax.random.normal(key_common, (D, KVW), jnp.float32), -4.0, 4.0) * col_scale
    own = jnp.clip(jax.random.normal(key_own, (N_DP, D, KVW), jnp.float32), -4.0, 4.0)
    return (common[None] + own).astype(jnp.bfloat16)


def levels(key, shape, cuts, low, largest):
    factor_of = 1.0
    for dim, shards_of in cuts:
        draws = jax.random.uniform(jax.random.fold_in(jax.random.fold_in(key, 6), dim), (shards_of,), jnp.float32, low / len(cuts), largest / len(cuts))
        factor_of = factor_of * jnp.repeat(jnp.exp(draws), shape[dim] // shards_of).reshape((-1,) + (1,) * (len(shape) - 1 - dim))
    return factor_of


def bell_draw(own_key, dims, width, bound, cuts=(), held_as=jnp.bfloat16):
    level = levels(own_key, dims, cuts, -0.22, 0.18) if cuts else 1.0
    array = jax.random.normal(own_key, dims, jnp.float32) * width * level
    return jnp.minimum(jnp.maximum(array, -bound), bound).astype(held_as)


def setup_inputs(seed: int = 0) -> dict:
    arg_keys = jax.random.split(jax.random.key(seed), 4)
    return {
        "grads": draw_grads(jax.random.fold_in(arg_keys[3], 71), 0),
        "error": bell_draw(arg_keys[1], (REPLICAS, D, KVW), 0.5, 4.0, ((0, 16), (2, 16)), jnp.float32),
        "q_prev": bell_draw(arg_keys[2], (KVW, RANK), 1.0, 5.0, ((0, 16),), jnp.float32),
    }


def reference(grads, error, q_prev):
    highest = lax.Precision.HIGHEST
    merged = grads.astype(jnp.float32) + error
    p_whole = jnp.einsum('rdk,kq->dq', merged, q_prev, precision=highest)
    gram = jnp.dot(p_whole.T, p_whole, precision=highest)
    lower = jnp.linalg.cholesky(gram)
    basis = lax.linalg.triangular_solve(lower, p_whole, left_side=False, lower=True, transpose_a=True)
    q_new = jnp.einsum('rdk,dq->kq', merged, basis, precision=highest) / REPLICAS
    approx = jnp.dot(basis, q_new.T, precision=highest)
    synced = approx.astype(jnp.bfloat16)
    error_out = merged - approx[None]
    return (synced, error_out, q_new)
```

```python
import jax
import jax.numpy as jnp
from jax import lax
from jax.experimental import pallas as pl
from jax.experimental.pallas import tpu as pltpu
from jax.sharding import PartitionSpec as P

MESH = pl.DeviceIdType.MESH
F32, BF16 = jnp.float32, jnp.bfloat16
D, COLS, RANK = 8192, 128, 32
X, Y, Z = 4, 4, 8
LANES = 128
BLOCKS = D // LANES
HALF = BLOCKS // 2
PIECE = HALF // (X * Y)
CHUNK = 1024
NCHUNK = D // CHUNK
PER = CHUNK // LANES
OFFSETS = sorted(
    [(i, j) for j in range(Y) for i in range(X) if (i, j) != (0, 0)],
    key=lambda o: -(min(o[0], X - o[0]) + min(o[1], Y - o[1])),
)
NT = (((1,), (1,)), ((), ()))
TN = (((0,), (0,)), ((), ()))


def dot(a, b, dims=(((1,), (0,)), ((), ())), precision=None):
    return lax.dot_general(a, b, dims, precision=precision, preferred_element_type=F32)


def pair(value):
    hi = value.astype(BF16)
    return hi, (value - hi.astype(F32)).astype(BF16)


def quarters(value, rows, columns):
    return (
        value[:rows, :columns]
        + value[:rows, columns:]
        + value[rows:, :columns]
        + value[rows:, columns:]
    )


def inverse_factor(gram):
    n = gram.shape[0]
    row = lax.broadcasted_iota(jnp.int32, (n, n), 0)
    col = lax.broadcasted_iota(jnp.int32, (n, n), 1)
    left, right = gram, jnp.where(row == col, 1.0, 0.0).astype(F32)
    for k in range(n):
        scale = left[:, k : k + 1] / left[k : k + 1, k : k + 1]
        scale = jnp.where(row[:, :1] > k, scale, 0.0)
        left, right = (
            left - scale * left[k : k + 1, :],
            right - scale * right[k : k + 1, :],
        )
    pivots = jnp.sum(jnp.where(row == col, left, 0.0), axis=1, keepdims=True)
    return right / jnp.sqrt(pivots)


def share_kernel(
    q_ref, g_hbm, e_hbm, merged, p_rows, linv_ref, terms_ref,
    g_in, e_in, pairs, part, sib, summed, from_xy, from_z, p_all, p_pairs, from_zt, t_mine, t_sib,
    ld_g, ld_e, sib_s, sib_r, xy_s, xy_r, z_s, z_r, ag_s, ag_r, fw_s, fw_r, tz_s, tz_r, tc_s, tc_r,
):
    dp, me = lax.axis_index("dp"), lax.axis_index("tensor")
    x, y = lax.rem(me, X), lax.div(me, X)
    z, core = lax.div(dp, 2), lax.rem(dp, 2)
    other = 1 - core

    def at_xy(dx, dy):
        return lax.rem(y + dy, Y) * X + lax.rem(x + dx, X)

    def at_z(dz):
        return lax.rem(z + dz, Z)

    sibling = (z * 2 + other, me)

    loads = []
    for i in range(NCHUNK):
        where = (other if i < NCHUNK // 2 else core) * (NCHUNK // 2) + i % (NCHUNK // 2)
        rows = pl.ds(pl.multiple_of(where * CHUNK, CHUNK), CHUNK)
        pair_of = (
            pltpu.make_async_copy(g_hbm.at[0, rows], g_in.at[rows], ld_g.at[i]),
            pltpu.make_async_copy(e_hbm.at[0, rows], e_in.at[rows], ld_e.at[i]),
        )
        for c in pair_of:
            c.start()
        loads.append((where, pair_of))

    barrier = pltpu.get_barrier_semaphore()
    pl.semaphore_signal(barrier, inc=1, device_id=sibling, device_id_type=MESH)
    for dx, dy in OFFSETS:
        pl.semaphore_signal(barrier, inc=1, device_id=(dp, at_xy(dx, dy)), device_id_type=MESH)
    for k in range(1, Z):
        pl.semaphore_signal(barrier, inc=1, device_id=(at_z(k) * 2 + core, me), device_id_type=MESH)

    qh, ql = pair(q_ref[...])
    q_pairs = jnp.concatenate(
        [jnp.concatenate([qh, qh], axis=1), jnp.concatenate([ql, ql], axis=1)], axis=0
    )

    def partial(i):
        where, pair_of = loads[i]
        for c in pair_of:
            c.wait()
        base = where * CHUNK

        def tile(j, _):
            rows = pl.ds(pl.multiple_of(base + j * 256, 256), 256)
            total = g_in[rows].astype(F32) + e_in[rows]
            merged[rows] = total
            hi, lo = pair(total)
            both = jnp.concatenate([hi, lo], axis=1)
            pairs[rows] = both
            out = dot(q_pairs, both, NT)
            out = out[:RANK] + out[RANK:]
            first = where * PER + j * 2
            part[first] = out[:, :LANES]
            part[first + 1] = out[:, LANES:]
            return 0

        lax.fori_loop(0, CHUNK // 256, tile, 0, unroll=True)

    for i in range(NCHUNK // 2):
        partial(i)
    pl.semaphore_wait(barrier, 1 + len(OFFSETS) + Z - 1)

    def to_sibling(i):
        return pltpu.make_async_remote_copy(
            src_ref=part.at[pl.ds(other * HALF + i * PER, PER)], dst_ref=sib.at[pl.ds(i * PER, PER)],
            send_sem=sib_s.at[i], recv_sem=sib_r.at[i], device_id=sibling, device_id_type=MESH,
        )

    for i in range(NCHUNK // 2):
        to_sibling(i).start()
    for i in range(NCHUNK // 2, NCHUNK):
        partial(i)
    for i in range(NCHUNK // 2):
        to_sibling(i).wait()

    def scatter(j):
        to = at_xy(*OFFSETS[j])
        return to, pltpu.make_async_remote_copy(
            src_ref=summed.at[pl.ds(to * PIECE, PIECE)], dst_ref=from_xy.at[j],
            send_sem=xy_s.at[j], recv_sem=xy_r.at[j], device_id=(dp, to), device_id_type=MESH,
        )

    for j in range(len(OFFSETS)):
        to, copy = scatter(j)
        piece = pl.ds(to * PIECE, PIECE)
        summed[piece] = part[pl.ds(core * HALF + to * PIECE, PIECE)] + sib[piece]
        copy.start()
    own = pl.ds(me * PIECE, PIECE)
    mine = pl.ds(core * HALF + me * PIECE, PIECE)
    total = part[mine] + sib[own]
    for j in reversed(range(len(OFFSETS))):
        scatter(j)[1].wait()
        total = total + from_xy[j]
    from_z[z] = total

    def along_z(k, buffer, s, r):
        to = at_z(k)
        return to, pltpu.make_async_remote_copy(
            src_ref=buffer.at[z], dst_ref=buffer.at[z],
            send_sem=s.at[k], recv_sem=r.at[z], device_id=(to * 2 + core, me), device_id_type=MESH,
        )

    def z_arrived(k, buffer, s, r):
        origin = at_z(k)
        pltpu.make_async_remote_copy(
            src_ref=buffer.at[origin], dst_ref=buffer.at[origin],
            send_sem=s.at[k], recv_sem=r.at[origin], device_id=(origin * 2 + core, me), device_id_type=MESH,
        ).wait_recv()

    z_order = (4, 3, 5, 2, 6, 1, 7)
    for k in z_order:
        along_z(k, from_z, z_s, z_r)[1].start()
    for k in reversed(z_order):
        z_arrived(k, from_z, z_s, z_r)
    total = from_z[0]
    for k in range(1, Z):
        total = total + from_z[k]
    p_all[mine] = total

    def gather(j):
        return pltpu.make_async_remote_copy(
            src_ref=p_all.at[mine], dst_ref=p_all.at[mine],
            send_sem=ag_s.at[j], recv_sem=ag_r.at[j], device_id=(dp, at_xy(*OFFSETS[j])), device_id_type=MESH,
        )

    def forward(j, half):
        dx, dy = OFFSETS[j] if j < len(OFFSETS) else (0, 0)
        piece = pl.ds(half * HALF + at_xy(X - dx, Y - dy) * PIECE, PIECE)
        return pltpu.make_async_remote_copy(
            src_ref=p_all.at[piece], dst_ref=p_all.at[piece],
            send_sem=fw_s.at[j], recv_sem=fw_r.at[j], device_id=sibling, device_id_type=MESH,
        )

    def gathered(j):
        dx, dy = OFFSETS[j]
        piece = pl.ds(core * HALF + at_xy(X - dx, Y - dy) * PIECE, PIECE)
        pltpu.make_async_remote_copy(
            src_ref=p_all.at[piece], dst_ref=p_all.at[piece],
            send_sem=ag_s.at[j], recv_sem=ag_r.at[j], device_id=(dp, at_xy(dx, dy)), device_id_type=MESH,
        ).wait_recv()

    for j in range(len(OFFSETS)):
        gather(j).start()
    forward(len(OFFSETS), core).start()
    for j in reversed(range(len(OFFSETS))):
        gathered(j)
        forward(j, core).start()

    def terms(half, acc):
        def step(i, acc):
            chunk = half * (NCHUNK // 2) + i
            blocks = p_all[pl.ds(chunk * PER, PER)]
            hi, lo = pair(jnp.concatenate([blocks[b] for b in range(PER)], axis=1))
            both = jnp.concatenate([hi, lo], axis=0)
            p_pairs[chunk] = both
            rows = pl.ds(pl.multiple_of(chunk * CHUNK, CHUNK), CHUNK)
            return acc + dot(both, pairs[rows])

        return lax.fori_loop(0, NCHUNK // 2, step, acc)

    acc = terms(core, jnp.zeros((2 * RANK, 2 * COLS), F32))
    for j in reversed(range(len(OFFSETS) + 1)):
        forward(j, other).wait_recv()
    acc = terms(other, acc)
    from_zt[z] = quarters(acc, RANK, COLS)
    for k in z_order:
        along_z(k, from_zt, tz_s, tz_r)[1].start()

    def gram_step(i, acc):
        both = p_pairs[i]
        return acc + dot(both, both, NT)

    gram = lax.fori_loop(0, NCHUNK, gram_step, jnp.zeros((2 * RANK, 2 * RANK), F32))
    linv_ref[...] = inverse_factor(quarters(gram, RANK, RANK))

    def turn(b, _):
        block = p_all[b]
        hi = block.astype(BF16).astype(F32)
        lo = block - hi
        stacked = jnp.concatenate([hi, lo, hi, lo], axis=0)
        p_rows[pl.ds(pl.multiple_of(b * LANES, LANES), LANES)] = stacked.T.astype(BF16)
        return 0

    lax.fori_loop(0, BLOCKS, turn, 0, unroll=4)

    for k in reversed(z_order):
        z_arrived(k, from_zt, tz_s, tz_r)
    total = from_zt[0]
    for k in range(1, Z):
        total = total + from_zt[k]
    t_mine[...] = total
    last = pltpu.make_async_remote_copy(
        src_ref=t_mine, dst_ref=t_sib, send_sem=tc_s, recv_sem=tc_r, device_id=sibling, device_id_type=MESH
    )
    last.start()
    for j in range(len(OFFSETS)):
        gather(j).wait_send()
    for j in range(len(OFFSETS) + 1):
        forward(j, core).wait_send()
    for k in z_order:
        along_z(k, from_z, z_s, z_r)[1].wait_send()
        along_z(k, from_zt, tz_s, tz_r)[1].wait_send()
    last.wait()
    terms_ref[...] = t_mine[...] + t_sib[...]


def share(q_t, grads, error):
    sems = pltpu.SemaphoreType.DMA
    n = len(OFFSETS)
    return pl.pallas_call(
        share_kernel,
        name="share",
        out_shape=(
            pltpu.VMEM((D, COLS), F32),
            pltpu.VMEM((D, LANES), BF16),
            pltpu.VMEM((RANK, RANK), F32),
            pltpu.VMEM((RANK, COLS), F32),
        ),
        in_specs=[
            pl.BlockSpec(memory_space=pltpu.VMEM),
            pl.BlockSpec(memory_space=pltpu.HBM),
            pl.BlockSpec(memory_space=pltpu.HBM),
        ],
        out_specs=[pl.BlockSpec(memory_space=pltpu.VMEM)] * 4,
        scratch_shapes=[
            pltpu.VMEM((D, COLS), BF16),
            pltpu.VMEM((D, COLS), F32),
            pltpu.VMEM((D, 2 * COLS), BF16),
            pltpu.VMEM((BLOCKS, RANK, LANES), F32),
            pltpu.VMEM((HALF, RANK, LANES), F32),
            pltpu.VMEM((HALF, RANK, LANES), F32),
            pltpu.VMEM((n, PIECE, RANK, LANES), F32),
            pltpu.VMEM((Z, PIECE, RANK, LANES), F32),
            pltpu.VMEM((BLOCKS, RANK, LANES), F32),
            pltpu.VMEM((NCHUNK, 2 * RANK, CHUNK), BF16),
            pltpu.VMEM((Z, RANK, COLS), F32),
            pltpu.VMEM((RANK, COLS), F32),
            pltpu.VMEM((RANK, COLS), F32),
            sems((NCHUNK,)), sems((NCHUNK,)),
            sems((NCHUNK // 2,)), sems((NCHUNK // 2,)),
            sems((n,)), sems((n,)),
            sems((Z,)), sems((Z,)),
            sems((n,)), sems((n,)),
            sems((n + 1,)), sems((n + 1,)),
            sems((Z,)), sems((Z,)),
            sems, sems,
        ],
        compiler_params=pltpu.CompilerParams(
            collective_id=0, has_side_effects=True, vmem_limit_bytes=32 * 1024 * 1024
        ),
    )(q_t, *(pltpu.with_memory_space_constraint(a, pltpu.HBM) for a in (grads, error)))


def finish_kernel(replicas, merged, p_rows, linv_ref, terms_ref, synced, error_out, q_ref, out, rows_out, sem, sem_rows):
    dp = lax.axis_index("dp")
    linv = linv_ref[...]
    highest = lax.Precision.HIGHEST
    q_t = dot(linv, terms_ref[...], precision=highest) / replicas
    q_ref[...] = q_t
    hi, lo = pair(dot(linv, q_t, TN, precision=highest))
    right = jnp.concatenate([hi, hi, lo, lo], axis=0)
    copies = []
    for i in range(NCHUNK):
        rows = pl.ds(i * CHUNK, CHUNK)
        out[rows] = merged[rows] - dot(p_rows[rows], right)
        copies.append(pltpu.make_async_copy(out.at[rows], error_out.at[0, rows], sem.at[i]))
        copies[-1].start()
    own = D // replicas
    rows_out[...] = dot(p_rows[pl.ds(pl.multiple_of(dp * own, own), own)], right).astype(BF16)
    copies.append(pltpu.make_async_copy(rows_out, synced, sem_rows))
    copies[-1].start()
    for c in copies:
        c.wait()


def finish(replicas, merged, p_rows, linv, terms):
    def body(*refs):
        finish_kernel(replicas, *refs)

    sems = pltpu.SemaphoreType.DMA
    own = D // replicas
    args = [pltpu.with_memory_space_constraint(a, pltpu.VMEM) for a in (merged, p_rows, linv, terms)]
    return pl.pallas_call(
        body,
        name="finish",
        out_shape=(
            jax.ShapeDtypeStruct((own, COLS), BF16),
            jax.ShapeDtypeStruct((1, D, COLS), F32),
            jax.ShapeDtypeStruct((RANK, COLS), F32),
        ),
        in_specs=[pl.BlockSpec(memory_space=pltpu.VMEM)] * 4,
        out_specs=[
            pl.BlockSpec(memory_space=pl.ANY),
            pl.BlockSpec(memory_space=pl.ANY),
            pl.BlockSpec(memory_space=pltpu.VMEM),
        ],
        scratch_shapes=[
            pltpu.VMEM((D, COLS), F32),
            pltpu.VMEM((own, COLS), BF16),
            sems((NCHUNK,)),
            sems,
        ],
        compiler_params=pltpu.CompilerParams(vmem_limit_bytes=16 * 1024 * 1024),
    )(*args)


def solution(mesh):
    replicas = mesh.shape["dp"]

    def on_device(grads, error, q_prev):
        merged, p_rows, linv, terms = share(q_prev.T, grads, error)
        synced, error_out, q_t = finish(replicas, merged, p_rows, linv, terms)
        return synced, error_out, q_t.T

    placed = (P("dp", None, "tensor"), P("dp", None, "tensor"), P("tensor", None))
    return jax.shard_map(
        on_device,
        mesh=mesh,
        in_specs=placed,
        out_specs=(P("dp", "tensor"), P("dp", None, "tensor"), P("tensor", None)),
        check_vma=False,
    )
```

```python
import jax
import jax.numpy as jnp
from jax import lax
from jax.experimental import pallas as pl
from jax.experimental.pallas import tpu as pltpu
from jax.sharding import PartitionSpec as P

MESH = pl.DeviceIdType.MESH
F32, BF16 = jnp.float32, jnp.bfloat16
D, COLS, RANK = 8192, 128, 32
X, Y, Z = 4, 4, 8
GROUPS = COLS // RANK
ROWS = D // GROUPS
HALF = ROWS // 2
CHUNK = 512
NC = HALF // CHUNK
UNIT = 512
STREAMS = (("xy", 48), ("z", 32))
PLANE = sorted(
    [(i, j) for j in range(Y) for i in range(X) if (i, j) != (0, 0)],
    key=lambda o: -(min(o[0], X - o[0]) + min(o[1], Y - o[1])),
)
LINE = (4, 3, 5, 2, 6, 1, 7)
MEMBERS = {"xy": X * Y, "z": Z}
OTHER = {"xy": "z", "z": "xy"}
NN = (((1,), (0,)), ((), ()))
NT = (((1,), (1,)), ((), ()))
TN = (((0,), (0,)), ((), ()))


def dot(a, b, dims=NN, precision=None):
    return lax.dot_general(a, b, dims, precision=precision, preferred_element_type=F32)


def pair(value):
    hi = value.astype(BF16)
    return hi, (value - hi.astype(F32)).astype(BF16)


def quarters(value, rows, columns):
    return (
        value[:rows, :columns]
        + value[:rows, columns:]
        + value[rows:, :columns]
        + value[rows:, columns:]
    )


def inverse_factor(gram):
    n = gram.shape[0]
    row = lax.broadcasted_iota(jnp.int32, (n, n), 0)
    col = lax.broadcasted_iota(jnp.int32, (n, n), 1)
    left, right = gram, jnp.where(row == col, 1.0, 0.0).astype(F32)
    for k in range(n):
        scale = left[:, k : k + 1] / left[k : k + 1, k : k + 1]
        scale = jnp.where(row[:, :1] > k, scale, 0.0)
        left, right = (
            left - scale * left[k : k + 1, :],
            right - scale * right[k : k + 1, :],
        )
    pivots = jnp.sum(jnp.where(row == col, left, 0.0), axis=1, keepdims=True)
    return right / jnp.sqrt(pivots)


def share_kernel(
    q_hbm, g_hbm, e_hbm, merged, p_pair, linv_ref, ginv_ref, terms_ref,
    q_in, g_in, e_in, part, sib, summed, p_all, m_sib, s_pair, from_zt, t_mine, t_sib,
    g_mine, g_sib, ld_q, ld_g, ld_e, sib_s, sib_r, m_s, m_r, fw_s, fw_r, tz_s, tz_r, tc_s, tc_r, g_s, g_r, *per_stream,
):
    dp, me = lax.axis_index("dp"), lax.axis_index("tensor")
    x, y = lax.rem(me, X), lax.div(me, X)
    z, core = lax.div(dp, 2), lax.rem(dp, 2)
    other = 1 - core
    sibling = (z * 2 + other, me)
    hisrow, myrow = other * HALF, core * HALF
    place = {"xy": me, "z": z}
    offsets = {"xy": PLANE, "z": LINE}

    def member(axes, offset, back=False):
        if axes == "z":
            return lax.rem(z + (Z - offset if back else offset), Z)
        dx, dy = (X - offset[0], Y - offset[1]) if back else offset
        return lax.rem(y + dy, Y) * X + lax.rem(x + dx, X)

    def device(axes, index):
        return (dp, index) if axes == "xy" else (index * 2 + core, me)

    def remote(src, dst, send, recv, to):
        return pltpu.make_async_remote_copy(
            src_ref=src, dst_ref=dst, send_sem=send, recv_sem=recv, device_id=to, device_id_type=MESH
        )

    def rows_of(start, size):
        return pl.ds(pl.multiple_of(start, 8), size)

    load_q = pltpu.make_async_copy(q_hbm, q_in, ld_q)
    load_q.start()
    loads = []
    for i in range(2 * NC):
        rows = rows_of((hisrow if i < NC else myrow) + (i % NC) * CHUNK, CHUNK)
        both = (
            pltpu.make_async_copy(g_hbm.at[:, rows], g_in.at[:, rows], ld_g.at[i]),
            pltpu.make_async_copy(e_hbm.at[:, rows], e_in.at[:, rows], ld_e.at[i]),
        )
        for c in both:
            c.start()
        loads.append(both)

    barrier = pltpu.get_barrier_semaphore()
    pl.semaphore_signal(barrier, inc=1, device_id=sibling, device_id_type=MESH)
    for axes in ("xy", "z"):
        for o in offsets[axes]:
            pl.semaphore_signal(barrier, inc=1, device_id=device(axes, member(axes, o)), device_id_type=MESH)

    load_q.wait()
    qh, ql = pair(q_in[...])
    q_left = jnp.concatenate(
        [jnp.concatenate([qh, qh], axis=1), jnp.concatenate([ql, ql], axis=1)], axis=0
    )

    def partial(i):
        for c in loads[i]:
            c.wait()
        first = (hisrow if i < NC else myrow) + (i % NC) * CHUNK
        rows = rows_of(first, CHUNK)
        for g in range(GROUPS):
            total = g_in[g, rows].astype(F32) + e_in[g, rows]
            merged[g, rows] = total
            out = dot(q_left, jnp.concatenate(pair(total), axis=1), NT)
            out = out[:RANK] + out[RANK:]
            for b in range(CHUNK // COLS):
                part[rows_of(first + b * COLS + g * RANK, RANK)] = out[:, b * COLS : (b + 1) * COLS]

    def to_sibling(i):
        return remote(part.at[rows_of(hisrow + i * CHUNK, CHUNK)], sib.at[pl.ds(i * CHUNK, CHUNK)],
                      sib_s.at[i], sib_r.at[i], sibling)

    def m_to_sibling(g):
        return remote(merged.at[g, rows_of(hisrow, HALF)], m_sib.at[g], m_s, m_r, sibling)

    for i in range(NC):
        partial(i)
        if i == 0:
            pl.semaphore_wait(barrier, X * Y + Z - 1)
        to_sibling(i).start()
    for g in range(GROUPS):
        m_to_sibling(g).start()
    for i in range(NC):
        partial(NC + i)
    for i in range(NC):
        to_sibling(i).wait_recv()
        at = pl.ds(i * CHUNK, CHUNK)
        summed[at] = part[rows_of(myrow + i * CHUNK, CHUNK)] + sib[at]

    streams = []
    base = 0
    for n, (axes, size) in enumerate(STREAMS):
        streams.append((axes, size, base, *per_stream[8 * n : 8 * n + 8]))
        base += MEMBERS[axes] * size
    assert base == HALF

    def scatter(stream, j):
        axes, size, base, inbox, _, s1, r1, *_ = stream
        to = member(axes, offsets[axes][j])
        return remote(summed.at[rows_of(base + to * size, size)], inbox.at[j], s1, r1, device(axes, to))

    def exchange(stream, j):
        axes, size, base, _, box, _, _, s2, r2, _, _ = stream
        axes = OTHER[axes]
        mine = box.at[place[axes]]
        return remote(mine, mine, s2, r2, device(axes, member(axes, offsets[axes][j])))

    def gather(stream, j):
        axes, size, base, *_, s3, r3 = stream
        piece = p_all.at[rows_of(myrow + base + place[axes] * size, size)]
        return remote(piece, piece, s3, r3, device(axes, member(axes, offsets[axes][j])))

    def whole(stream, step):
        axes, size, base, inbox, box, s1, r1, s2, r2, s3, r3 = stream
        n = count(stream, step)
        what = inbox if step == 1 else box.at[pl.ds(0, n)] if step == 2 else p_all.at[pl.ds(0, n * size)]
        send, recv = ((s1, r1), (s2, r2), (s3, r3))[step - 1]
        return remote(what, what, send, recv, sibling)

    def count(stream, step):
        return MEMBERS[OTHER[stream[0]] if step == 2 else stream[0]] - 1

    for j in range(X * Y - 1):
        for stream in streams:
            if j < count(stream, 1):
                scatter(stream, j).start()

    for stream in streams:
        axes, size, base, inbox, box, *_ = stream
        total = summed[rows_of(base + place[axes] * size, size)]
        whole(stream, 1).wait_recv()
        for j in range(count(stream, 1)):
            total = total + inbox[j]
        box[place[OTHER[axes]]] = total
        for j in range(count(stream, 2)):
            exchange(stream, j).start()

    all_m = remote(m_sib, m_sib, m_s, m_r, sibling)
    all_m.wait_recv()

    def chip_pairs(i, _):
        at = pl.ds(pl.multiple_of(i * UNIT, UNIT), UNIT)
        for g in range(GROUPS):
            hi, lo = pair(merged[g, rows_of(myrow + i * UNIT, UNIT)] + m_sib[g, at])
            s_pair[g, at] = jnp.concatenate([hi, lo], axis=1)
        return 0

    lax.fori_loop(0, HALF // UNIT, chip_pairs, 0)

    for stream in streams:
        axes, size, base, inbox, box, *_ = stream
        whole(stream, 2).wait_recv()
        total = box[0]
        for j in range(1, MEMBERS[OTHER[axes]]):
            total = total + box[j]
        p_all[rows_of(myrow + base + place[axes] * size, size)] = total
        for j in range(count(stream, 3)):
            gather(stream, j).start()

    for stream in streams:
        whole(stream, 3).wait_recv()

    def forward(base):
        half = p_all.at[rows_of(base, HALF)]
        return remote(half, half, fw_s, fw_r, sibling)

    forward(myrow).start()

    def turned(base):
        blocks = [p_all[rows_of(base + b * COLS, COLS)] for b in range(HALF // COLS)]
        return blocks, pair(jnp.concatenate(blocks, axis=1))

    def store_rows(base, blocks):
        for b, block in enumerate(blocks):
            p_pair[rows_of(base + b * COLS, COLS)] = jnp.concatenate(pair(block.T), axis=1)

    blocks, halves = turned(myrow)
    left = [
        jnp.concatenate([v[g * RANK : (g + 1) * RANK] for g in range(GROUPS)], axis=1) for v in halves
    ]
    acc = dot(jnp.concatenate(left, axis=0), s_pair[...].reshape(GROUPS * HALF, 2 * COLS))
    from_zt[z] = quarters(acc, RANK, COLS)

    def terms_along(j):
        to = member("z", LINE[j])
        return remote(from_zt.at[z], from_zt.at[z], tz_s, tz_r, device("z", to))

    others = from_zt.at[pl.ds(0, Z - 1)]
    all_terms = remote(others, others, tz_s, tz_r, sibling)

    for j in range(Z - 1):
        terms_along(j).start()

    both = jnp.concatenate(halves, axis=0)
    gram = quarters(dot(both, both, NT), COLS, COLS)
    small = gram[:RANK, :RANK]
    for g in range(1, GROUPS):
        small = small + gram[g * RANK : (g + 1) * RANK, g * RANK : (g + 1) * RANK]
    g_mine[...] = small
    swap = remote(g_mine, g_sib, g_s, g_r, sibling)
    swap.start()
    store_rows(myrow, blocks)
    swap.wait()
    small = g_mine[...] + g_sib[...]
    linv = inverse_factor(small)
    linv_ref[...] = linv
    ginv_ref[...] = dot(linv, linv, TN, lax.Precision.HIGHEST)
    forward(hisrow).wait_recv()
    store_rows(hisrow, turned(hisrow)[0])

    for i in range(NC):
        to_sibling(i).wait_send()
    all_m.wait_send()
    for stream in streams:
        for step in (1, 2, 3):
            whole(stream, step).wait_send()
    forward(myrow).wait_send()

    all_terms.wait_recv()
    total = from_zt[0]
    for k in range(1, Z):
        total = total + from_zt[k]
    t_mine[...] = total
    last = remote(t_mine, t_sib, tc_s, tc_r, sibling)
    last.start()
    all_terms.wait_send()
    last.wait()
    terms_ref[...] = t_mine[...] + t_sib[...]


def share(q_t, grads, error):
    sems = pltpu.SemaphoreType.DMA
    hbm = pl.BlockSpec(memory_space=pltpu.HBM)
    args = (q_t, grads.reshape(GROUPS, ROWS, COLS), error.reshape(GROUPS, ROWS, COLS))
    per_stream = []
    for axes, size in STREAMS:
        first, second = MEMBERS[axes], MEMBERS[OTHER[axes]]
        per_stream += [
            pltpu.VMEM((first - 1, size, COLS), F32),
            pltpu.VMEM((second, size, COLS), F32),
            sems, sems, sems, sems, sems, sems,
        ]
    return pl.pallas_call(
        share_kernel,
        name="share",
        out_shape=(
            pltpu.VMEM((GROUPS, ROWS, COLS), F32),
            pltpu.VMEM((ROWS, 2 * COLS), BF16),
            pltpu.VMEM((RANK, RANK), F32),
            pltpu.VMEM((RANK, RANK), F32),
            pltpu.VMEM((RANK, COLS), F32),
        ),
        in_specs=[hbm] * 3,
        out_specs=[pl.BlockSpec(memory_space=pltpu.VMEM)] * 5,
        scratch_shapes=[
            pltpu.VMEM((RANK, COLS), F32),
            pltpu.VMEM((GROUPS, ROWS, COLS), BF16),
            pltpu.VMEM((GROUPS, ROWS, COLS), F32),
            pltpu.VMEM((ROWS, COLS), F32),
            pltpu.VMEM((HALF, COLS), F32),
            pltpu.VMEM((HALF, COLS), F32),
            pltpu.VMEM((ROWS, COLS), F32),
            pltpu.VMEM((GROUPS, HALF, COLS), F32),
            pltpu.VMEM((GROUPS, HALF, 2 * COLS), BF16),
            pltpu.VMEM((Z, RANK, COLS), F32),
            pltpu.VMEM((RANK, COLS), F32),
            pltpu.VMEM((RANK, COLS), F32),
            pltpu.VMEM((RANK, RANK), F32),
            pltpu.VMEM((RANK, RANK), F32),
            sems, sems((2 * NC,)), sems((2 * NC,)),
            sems((NC,)), sems((NC,)), sems, sems, sems, sems,
            sems, sems, sems, sems, sems, sems,
            *per_stream,
        ],
        compiler_params=pltpu.CompilerParams(
            collective_id=0, has_side_effects=True, vmem_limit_bytes=32 * 1024 * 1024
        ),
    )(*(pltpu.with_memory_space_constraint(a, pltpu.HBM) for a in args))


def finish_kernel(
    replicas, merged, p_pair, linv_ref, ginv_ref, terms_ref, synced, error_out, q_ref, right, out, rows_out, sem, sem_rows
):
    dp = lax.axis_index("dp")
    highest = lax.Precision.HIGHEST
    right[...] = jnp.zeros_like(right)
    terms = terms_ref[...] / replicas
    hi, lo = pair(dot(ginv_ref[...], terms, precision=highest))
    both = jnp.concatenate([hi, lo], axis=1)
    for g in range(GROUPS):
        right[g, pl.ds(g * RANK, RANK)] = both
        right[g, pl.ds(COLS + g * RANK, RANK)] = both

    def approx(g, rows):
        wide = dot(p_pair[rows], right[g])
        return wide[:, :COLS] + wide[:, COLS:]

    copies = []
    units = [(g, i * UNIT) for i in range(ROWS // UNIT) for g in range(GROUPS)]
    for n, (g, first) in enumerate(units):
        rows = pl.ds(first, UNIT)
        out[g, rows] = merged[g, rows] - approx(g, rows)
        copies.append(pltpu.make_async_copy(out.at[g, rows], error_out.at[g, rows], sem.at[n]))
        copies[-1].start()
        if n == len(units) // 2:
            own = D // replicas
            per = ROWS // own
            rows = pl.ds(pl.multiple_of(lax.rem(dp, per) * own, own), own)
            rows_out[...] = approx(lax.div(dp, per), rows).astype(BF16)
            copies.append(pltpu.make_async_copy(rows_out, synced, sem_rows))
            copies[-1].start()
    q_ref[...] = dot(linv_ref[...], terms, precision=highest)
    for c in copies:
        c.wait()


def finish(replicas, *operands):
    def body(*refs):
        finish_kernel(replicas, *refs)

    sems = pltpu.SemaphoreType.DMA
    own = D // replicas
    vmem, hbm = pl.BlockSpec(memory_space=pltpu.VMEM), pl.BlockSpec(memory_space=pl.ANY)
    return pl.pallas_call(
        body,
        name="finish",
        out_shape=(
            jax.ShapeDtypeStruct((own, COLS), BF16),
            jax.ShapeDtypeStruct((GROUPS, ROWS, COLS), F32),
            jax.ShapeDtypeStruct((RANK, COLS), F32),
        ),
        in_specs=[vmem] * 5,
        out_specs=[hbm, hbm, vmem],
        scratch_shapes=[
            pltpu.VMEM((GROUPS, 2 * COLS, 2 * COLS), BF16),
            pltpu.VMEM((GROUPS, ROWS, COLS), F32),
            pltpu.VMEM((own, COLS), BF16),
            sems((D // UNIT,)),
            sems,
        ],
        compiler_params=pltpu.CompilerParams(vmem_limit_bytes=16 * 1024 * 1024),
    )(*(pltpu.with_memory_space_constraint(a, pltpu.VMEM) for a in operands))


def solution(mesh):
    replicas = mesh.shape["dp"]

    def on_device(grads, error, q_prev):
        synced, error_out, q_t = finish(replicas, *share(q_prev.T, grads, error))
        return synced, error_out.reshape(1, D, COLS), q_t.T

    placed = (P("dp", None, "tensor"), P("dp", None, "tensor"), P("tensor", None))
    return jax.shard_map(
        on_device,
        mesh=mesh,
        in_specs=placed,
        out_specs=(P("dp", "tensor"), P("dp", None, "tensor"), P("tensor", None)),
        check_vma=False,
    )
```

```python
import jax
import jax.numpy as jnp
from jax import lax
from jax.experimental import pallas as pl
from jax.experimental.pallas import tpu as pltpu
from jax.sharding import PartitionSpec as P

MESH = pl.DeviceIdType.MESH
F32, BF16 = jnp.float32, jnp.bfloat16
D, COLS, RANK = 8192, 128, 32
X, Y, Z = 4, 4, 8
GROUPS = COLS // RANK
ROWS = D // GROUPS
HALF = ROWS // 2
CHUNK = 512
NC = HALF // CHUNK
UNIT = 512
STREAMS = (("z", 32), ("xy", 24), ("xy", 24))
PLANE = sorted(
    [(i, j) for j in range(Y) for i in range(X)],
    key=lambda o: -(min(o[0], X - o[0]) + min(o[1], Y - o[1])),
)
LINE = (4, 3, 5, 2, 6, 1, 7, 0)
MEMBERS = {"xy": X * Y, "z": Z}
OTHER = {"xy": "z", "z": "xy"}
NN = (((1,), (0,)), ((), ()))
NT = (((1,), (1,)), ((), ()))
TN = (((0,), (0,)), ((), ()))


def dot(a, b, dims=NN, precision=None):
    return lax.dot_general(a, b, dims, precision=precision, preferred_element_type=F32)


def pair(value):
    hi = value.astype(BF16)
    return hi, (value - hi.astype(F32)).astype(BF16)


def quarters(value, rows, columns):
    return (
        value[:rows, :columns]
        + value[:rows, columns:]
        + value[rows:, :columns]
        + value[rows:, columns:]
    )


def inverse_factor(gram):
    n = gram.shape[0]
    row = lax.broadcasted_iota(jnp.int32, (n, n), 0)
    col = lax.broadcasted_iota(jnp.int32, (n, n), 1)
    left, right = gram, jnp.where(row == col, 1.0, 0.0).astype(F32)
    for k in range(n):
        scale = left[:, k : k + 1] / left[k : k + 1, k : k + 1]
        scale = jnp.where(row[:, :1] > k, scale, 0.0)
        left, right = (
            left - scale * left[k : k + 1, :],
            right - scale * right[k : k + 1, :],
        )
    pivots = jnp.sum(jnp.where(row == col, left, 0.0), axis=1, keepdims=True)
    return right / jnp.sqrt(pivots)


def share_kernel(
    q_hbm, g_hbm, e_hbm, merged, p_pair, linv_ref, ginv_ref, terms_ref,
    q_in, g_in, e_in, part, sib, summed, p_all, m_sib, s_pair, from_zt, t_mine, t_sib, t_all,
    g_mine, g_sib, ld_q, ld_g, ld_e, sib_s, sib_r, m_s, m_r, fw_s, fw_r, tz_s, tz_r, tu_s, tu_r, td_s, td_r, g_s, g_r, *per_stream,
):
    dp, me = lax.axis_index("dp"), lax.axis_index("tensor")
    x, y = lax.rem(me, X), lax.div(me, X)
    z, core = lax.div(dp, 2), lax.rem(dp, 2)
    other = 1 - core
    sibling = (z * 2 + other, me)
    hisrow, myrow = other * HALF, core * HALF
    place = {"xy": me, "z": z}
    offsets = {"xy": PLANE, "z": LINE}

    def member(axes, offset, back=False):
        if axes == "z":
            return lax.rem(z + (Z - offset if back else offset), Z)
        dx, dy = (X - offset[0], Y - offset[1]) if back else offset
        return lax.rem(y + dy, Y) * X + lax.rem(x + dx, X)

    def device(axes, index):
        return (z * 2 + other, index) if axes == "xy" else (index * 2 + other, me)

    def remote(src, dst, send, recv, to):
        return pltpu.make_async_remote_copy(
            src_ref=src, dst_ref=dst, send_sem=send, recv_sem=recv, device_id=to, device_id_type=MESH
        )

    def rows_of(start, size):
        return pl.ds(pl.multiple_of(start, 8), size)

    load_q = pltpu.make_async_copy(q_hbm, q_in, ld_q)
    load_q.start()
    loads = []
    for i in range(2 * NC):
        rows = rows_of((hisrow if i < NC else myrow) + (i % NC) * CHUNK, CHUNK)
        both = (
            pltpu.make_async_copy(g_hbm.at[:, rows], g_in.at[:, rows], ld_g.at[i]),
            pltpu.make_async_copy(e_hbm.at[:, rows], e_in.at[:, rows], ld_e.at[i]),
        )
        for c in both:
            c.start()
        loads.append(both)

    barrier = pltpu.get_barrier_semaphore()
    greeted = [device("xy", member("xy", o)) for o in PLANE]
    for o in LINE[:-1]:
        greeted += [device("z", member("z", o)), (member("z", o) * 2 + core, me)]
    for to in greeted:
        pl.semaphore_signal(barrier, inc=1, device_id=to, device_id_type=MESH)

    load_q.wait()
    qh, ql = pair(q_in[...])
    q_left = jnp.concatenate(
        [jnp.concatenate([qh, qh], axis=1), jnp.concatenate([ql, ql], axis=1)], axis=0
    )

    def partial(i):
        for c in loads[i]:
            c.wait()
        first = (hisrow if i < NC else myrow) + (i % NC) * CHUNK
        rows = rows_of(first, CHUNK)
        for g in range(GROUPS):
            total = g_in[g, rows].astype(F32) + e_in[g, rows]
            merged[g, rows] = total
            out = dot(q_left, jnp.concatenate(pair(total), axis=1), NT)
            out = out[:RANK] + out[RANK:]
            for b in range(CHUNK // COLS):
                part[rows_of(first + b * COLS + g * RANK, RANK)] = out[:, b * COLS : (b + 1) * COLS]

    def to_sibling(i):
        return remote(part.at[rows_of(hisrow + i * CHUNK, CHUNK)], sib.at[pl.ds(i * CHUNK, CHUNK)],
                      sib_s.at[i], sib_r.at[i], sibling)

    def m_to_sibling(g):
        return remote(merged.at[g, rows_of(myrow, HALF)], m_sib.at[g], m_s, m_r, sibling)

    for i in range(NC):
        partial(i)
        if i == 0:
            pl.semaphore_wait(barrier, len(greeted))
        to_sibling(i).start()
    for i in range(NC):
        partial(NC + i)
    for g in range(GROUPS):
        m_to_sibling(g).start()
    for i in range(NC):
        to_sibling(i).wait_recv()
        at = pl.ds(i * CHUNK, CHUNK)
        summed[at] = part[rows_of(myrow + i * CHUNK, CHUNK)] + sib[at]

    streams = []
    base = 0
    for n, (axes, size) in enumerate(STREAMS):
        streams.append((axes, size, base, *per_stream[10 * n : 10 * n + 10]))
        base += MEMBERS[axes] * size
    assert base == HALF

    def count(stream, step):
        return MEMBERS[OTHER[stream[0]] if step == 2 else stream[0]]

    def scatter(stream, j):
        axes, size, base, inbox, _, _, _, s1, r1, *_ = stream
        to = member(axes, offsets[axes][j])
        return remote(summed.at[rows_of(base + to * size, size)], inbox.at[j], s1, r1, device(axes, to))

    def exchange(stream, j):
        axes, size, base, _, box, mid, _, _, _, s2, r2, _, _ = stream
        axes = OTHER[axes]
        return remote(mid, box.at[place[axes]], s2, r2, device(axes, member(axes, offsets[axes][j])))

    def gather(stream, j):
        axes, size, base, _, _, _, done, *_, s3, r3 = stream
        target = p_all.at[rows_of(myrow + base + place[axes] * size, size)]
        return remote(done, target, s3, r3, device(axes, member(axes, offsets[axes][j])))

    def whole(stream, step):
        axes, size, base, inbox, box, _, _, s1, r1, s2, r2, s3, r3 = stream
        what = inbox if step == 1 else box if step == 2 else p_all.at[pl.ds(0, count(stream, 3) * size)]
        send, recv = ((s1, r1), (s2, r2), (s3, r3))[step - 1]
        return remote(what, what, send, recv, sibling)

    for j in range(X * Y):
        for stream in streams:
            if j < count(stream, 1):
                scatter(stream, j).start()

    for stream in streams:
        axes, size, base, inbox, box, mid, *_ = stream
        whole(stream, 1).wait_recv()
        total = inbox[0]
        for j in range(1, count(stream, 1)):
            total = total + inbox[j]
        mid[...] = total
        for j in range(count(stream, 2)):
            exchange(stream, j).start()

    all_m = remote(m_sib, m_sib, m_s, m_r, sibling)
    all_m.wait_recv()

    def chip_pairs(i, _):
        at = pl.ds(pl.multiple_of(i * UNIT, UNIT), UNIT)
        for g in range(GROUPS):
            hi, lo = pair(merged[g, rows_of(hisrow + i * UNIT, UNIT)] + m_sib[g, at])
            s_pair[g, at] = jnp.concatenate([hi, lo], axis=1)
        return 0

    lax.fori_loop(0, HALF // UNIT, chip_pairs, 0)

    for stream in streams:
        axes, size, base, inbox, box, mid, done, *_ = stream
        whole(stream, 2).wait_recv()
        total = box[0]
        for j in range(1, count(stream, 2)):
            total = total + box[j]
        done[...] = total
        for j in range(count(stream, 3)):
            gather(stream, j).start()

    for stream in streams:
        whole(stream, 3).wait_recv()

    def forward(base):
        half = p_all.at[rows_of(base, HALF)]
        return remote(half, half, fw_s, fw_r, sibling)

    def turned(base):
        blocks = [p_all[rows_of(base + b * COLS, COLS)] for b in range(HALF // COLS)]
        return blocks, pair(jnp.concatenate(blocks, axis=1))

    def store_rows(base, blocks):
        for b, block in enumerate(blocks):
            p_pair[rows_of(base + b * COLS, COLS)] = jnp.concatenate(pair(block.T), axis=1)

    blocks, halves = turned(hisrow)
    left = [
        jnp.concatenate([v[g * RANK : (g + 1) * RANK] for g in range(GROUPS)], axis=1) for v in halves
    ]
    acc = dot(jnp.concatenate(left, axis=0), s_pair[...].reshape(GROUPS * HALF, 2 * COLS))
    t_mine[...] = quarters(acc, RANK, COLS)

    up = remote(t_mine, t_sib, tu_s, tu_r, sibling)

    @pl.when(core == 0)
    def _():
        up.start()

    both = jnp.concatenate(halves, axis=0)
    gram = quarters(dot(both, both, NT), COLS, COLS)
    small = gram[:RANK, :RANK]
    for g in range(1, GROUPS):
        small = small + gram[g * RANK : (g + 1) * RANK, g * RANK : (g + 1) * RANK]
    g_mine[...] = small
    swap = remote(g_mine, g_sib, g_s, g_r, sibling)
    swap.start()
    forward(hisrow).start()

    others = from_zt.at[pl.ds(0, Z - 1)]
    all_terms = remote(others, others, tz_s, tz_r, sibling)

    @pl.when(core == 1)
    def _():
        up.wait_recv()
        from_zt[z] = t_mine[...] + t_sib[...]
        for o in LINE[:-1]:
            remote(from_zt.at[z], from_zt.at[z], tz_s, tz_r, (member("z", o) * 2 + 1, me)).start()

    store_rows(hisrow, blocks)
    swap.wait()
    linv = inverse_factor(g_mine[...] + g_sib[...])
    linv_ref[...] = linv
    ginv_ref[...] = dot(linv, linv, TN, lax.Precision.HIGHEST)
    forward(myrow).wait_recv()
    store_rows(myrow, turned(myrow)[0])

    for i in range(NC):
        to_sibling(i).wait_send()
    all_m.wait_send()
    for stream in streams:
        for step in (1, 2, 3):
            whole(stream, step).wait_send()
    forward(hisrow).wait_send()

    down = remote(t_all, t_all, td_s, td_r, sibling)

    @pl.when(core == 1)
    def _():
        all_terms.wait_recv()
        total = from_zt[0]
        for k in range(1, Z):
            total = total + from_zt[k]
        t_all[...] = total
        down.start()
        all_terms.wait_send()
        down.wait_send()

    @pl.when(core == 0)
    def _():
        up.wait_send()
        down.wait_recv()

    terms_ref[...] = t_all[...]


def share(q_t, grads, error):
    sems = pltpu.SemaphoreType.DMA
    hbm = pl.BlockSpec(memory_space=pltpu.HBM)
    args = (q_t, grads.reshape(GROUPS, ROWS, COLS), error.reshape(GROUPS, ROWS, COLS))
    per_stream = []
    for axes, size in STREAMS:
        first, second = MEMBERS[axes], MEMBERS[OTHER[axes]]
        per_stream += [
            pltpu.VMEM((first, size, COLS), F32),
            pltpu.VMEM((second, size, COLS), F32),
            pltpu.VMEM((size, COLS), F32),
            pltpu.VMEM((size, COLS), F32),
            sems, sems, sems, sems, sems, sems,
        ]
    return pl.pallas_call(
        share_kernel,
        name="share",
        out_shape=(
            pltpu.VMEM((GROUPS, ROWS, COLS), F32),
            pltpu.VMEM((ROWS, 2 * COLS), BF16),
            pltpu.VMEM((RANK, RANK), F32),
            pltpu.VMEM((RANK, RANK), F32),
            pltpu.VMEM((RANK, COLS), F32),
        ),
        in_specs=[hbm] * 3,
        out_specs=[pl.BlockSpec(memory_space=pltpu.VMEM)] * 5,
        scratch_shapes=[
            pltpu.VMEM((RANK, COLS), F32),
            pltpu.VMEM((GROUPS, ROWS, COLS), BF16),
            pltpu.VMEM((GROUPS, ROWS, COLS), F32),
            pltpu.VMEM((ROWS, COLS), F32),
            pltpu.VMEM((HALF, COLS), F32),
            pltpu.VMEM((HALF, COLS), F32),
            pltpu.VMEM((ROWS, COLS), F32),
            pltpu.VMEM((GROUPS, HALF, COLS), F32),
            pltpu.VMEM((GROUPS, HALF, 2 * COLS), BF16),
            pltpu.VMEM((Z, RANK, COLS), F32),
            pltpu.VMEM((RANK, COLS), F32),
            pltpu.VMEM((RANK, COLS), F32),
            pltpu.VMEM((RANK, COLS), F32),
            pltpu.VMEM((RANK, RANK), F32),
            pltpu.VMEM((RANK, RANK), F32),
            sems, sems((2 * NC,)), sems((2 * NC,)),
            sems((NC,)), sems((NC,)), sems, sems, sems, sems,
            sems, sems, sems, sems, sems, sems, sems, sems,
            *per_stream,
        ],
        compiler_params=pltpu.CompilerParams(
            collective_id=0, has_side_effects=True, vmem_limit_bytes=32 * 1024 * 1024
        ),
    )(*(pltpu.with_memory_space_constraint(a, pltpu.HBM) for a in args))


def finish_kernel(
    replicas, merged, p_pair, linv_ref, ginv_ref, terms_ref, synced, error_out, q_ref, right, out, rows_out, sem, sem_rows
):
    dp = lax.axis_index("dp")
    highest = lax.Precision.HIGHEST
    right[...] = jnp.zeros_like(right)
    terms = terms_ref[...] / replicas
    hi, lo = pair(dot(ginv_ref[...], terms, precision=highest))
    both = jnp.concatenate([hi, lo], axis=1)
    for g in range(GROUPS):
        right[g, pl.ds(g * RANK, RANK)] = both
        right[g, pl.ds(COLS + g * RANK, RANK)] = both

    def approx(g, rows):
        wide = dot(p_pair[rows], right[g])
        return wide[:, :COLS] + wide[:, COLS:]

    copies = []
    units = [(g, i * UNIT) for i in range(ROWS // UNIT) for g in range(GROUPS)]
    for n, (g, first) in enumerate(units):
        rows = pl.ds(first, UNIT)
        out[g, rows] = merged[g, rows] - approx(g, rows)
        copies.append(pltpu.make_async_copy(out.at[g, rows], error_out.at[g, rows], sem.at[n]))
        copies[-1].start()
        if n == len(units) // 2:
            own = D // replicas
            per = ROWS // own
            rows = pl.ds(pl.multiple_of(lax.rem(dp, per) * own, own), own)
            rows_out[...] = approx(lax.div(dp, per), rows).astype(BF16)
            copies.append(pltpu.make_async_copy(rows_out, synced, sem_rows))
            copies[-1].start()
    q_ref[...] = dot(linv_ref[...], terms, precision=highest)
    for c in copies:
        c.wait()


def finish(replicas, *operands):
    def body(*refs):
        finish_kernel(replicas, *refs)

    sems = pltpu.SemaphoreType.DMA
    own = D // replicas
    vmem, hbm = pl.BlockSpec(memory_space=pltpu.VMEM), pl.BlockSpec(memory_space=pl.ANY)
    return pl.pallas_call(
        body,
        name="finish",
        out_shape=(
            jax.ShapeDtypeStruct((own, COLS), BF16),
            jax.ShapeDtypeStruct((GROUPS, ROWS, COLS), F32),
            jax.ShapeDtypeStruct((RANK, COLS), F32),
        ),
        in_specs=[vmem] * 5,
        out_specs=[hbm, hbm, vmem],
        scratch_shapes=[
            pltpu.VMEM((GROUPS, 2 * COLS, 2 * COLS), BF16),
            pltpu.VMEM((GROUPS, ROWS, COLS), F32),
            pltpu.VMEM((own, COLS), BF16),
            sems((D // UNIT,)),
            sems,
        ],
        compiler_params=pltpu.CompilerParams(vmem_limit_bytes=16 * 1024 * 1024),
    )(*(pltpu.with_memory_space_constraint(a, pltpu.VMEM) for a in operands))


def solution(mesh):
    replicas = mesh.shape["dp"]

    def on_device(grads, error, q_prev):
        synced, error_out, q_t = finish(replicas, *share(q_prev.T, grads, error))
        return synced, error_out.reshape(1, D, COLS), q_t.T

    placed = (P("dp", None, "tensor"), P("dp", None, "tensor"), P("tensor", None))
    return jax.shard_map(
        on_device,
        mesh=mesh,
        in_specs=placed,
        out_specs=(P("dp", "tensor"), P("dp", None, "tensor"), P("tensor", None)),
        check_vma=False,
    )
```

```python
import jax
import jax.numpy as jnp
from jax import lax
from jax.experimental import pallas as pl
from jax.experimental.pallas import tpu as pltpu
from jax.sharding import PartitionSpec as P

MESH = pl.DeviceIdType.MESH
F32, BF16 = jnp.float32, jnp.bfloat16
D, COLS, RANK = 8192, 128, 32
X, Y, Z = 4, 4, 8
GROUPS = COLS // RANK
ROWS = D // GROUPS
HALF = ROWS // 2
CHUNK = 1024
NC = HALF // CHUNK
UNIT = 512
STREAMS = (("z", 32), ("xy", 24), ("xy", 24))
PLANE = sorted(
    [(i, j) for j in range(Y) for i in range(X)],
    key=lambda o: -(min(o[0], X - o[0]) + min(o[1], Y - o[1])),
)
LINE = (4, 3, 5, 2, 6, 1, 7, 0)
MEMBERS = {"xy": X * Y, "z": Z}
OTHER = {"xy": "z", "z": "xy"}
NN = (((1,), (0,)), ((), ()))
NT = (((1,), (1,)), ((), ()))
TN = (((0,), (0,)), ((), ()))


def dot(a, b, dims=NN, precision=None):
    return lax.dot_general(a, b, dims, precision=precision, preferred_element_type=F32)


def pair(value):
    hi = value.astype(BF16)
    return hi, (value - hi.astype(F32)).astype(BF16)


def quarters(value, rows, columns):
    return (
        value[:rows, :columns]
        + value[:rows, columns:]
        + value[rows:, :columns]
        + value[rows:, columns:]
    )


def inverse_factor(gram):
    n = gram.shape[0]
    row = lax.broadcasted_iota(jnp.int32, (n, n), 0)
    col = lax.broadcasted_iota(jnp.int32, (n, n), 1)
    left, right = gram, jnp.where(row == col, 1.0, 0.0).astype(F32)
    for k in range(n):
        scale = left[:, k : k + 1] / left[k : k + 1, k : k + 1]
        scale = jnp.where(row[:, :1] > k, scale, 0.0)
        left, right = (
            left - scale * left[k : k + 1, :],
            right - scale * right[k : k + 1, :],
        )
    pivots = jnp.sum(jnp.where(row == col, left, 0.0), axis=1, keepdims=True)
    return right / jnp.sqrt(pivots)


def share_kernel(
    q_hbm, g_hbm, e_hbm, merged, p_pair, linv_ref, ginv_ref, terms_ref,
    q_in, g_in, e_in, part, sib, summed, p_all, m_sib, s_pair, from_zt, t_mine, t_sib, t_all,
    g_mine, g_sib, ld_q, ld_g, ld_e, sib_s, sib_r, m_s, m_r, fw_s, fw_r, tz_s, tz_r, tu_s, tu_r, td_s, td_r, g_s, g_r, *per_stream,
):
    dp, me = lax.axis_index("dp"), lax.axis_index("tensor")
    x, y = lax.rem(me, X), lax.div(me, X)
    z, core = lax.div(dp, 2), lax.rem(dp, 2)
    other = 1 - core
    sibling = (z * 2 + other, me)
    hisrow, myrow = other * HALF, core * HALF
    place = {"xy": me, "z": z}
    offsets = {"xy": PLANE, "z": LINE}

    def member(axes, offset, back=False):
        if axes == "z":
            return lax.rem(z + (Z - offset if back else offset), Z)
        dx, dy = (X - offset[0], Y - offset[1]) if back else offset
        return lax.rem(y + dy, Y) * X + lax.rem(x + dx, X)

    def device(axes, index):
        return (z * 2 + other, index) if axes == "xy" else (index * 2 + other, me)

    def remote(src, dst, send, recv, to):
        return pltpu.make_async_remote_copy(
            src_ref=src, dst_ref=dst, send_sem=send, recv_sem=recv, device_id=to, device_id_type=MESH
        )

    def rows_of(start, size):
        return pl.ds(pl.multiple_of(start, 8), size)

    barrier = pltpu.get_barrier_semaphore()
    greeted = [device("xy", member("xy", o)) for o in PLANE]
    for o in LINE[:-1]:
        greeted += [device("z", member("z", o)), (member("z", o) * 2 + core, me)]
    for to in greeted:
        pl.semaphore_signal(barrier, inc=1, device_id=to, device_id_type=MESH)

    load_q = pltpu.make_async_copy(q_hbm, q_in, ld_q)
    load_q.start()
    loads = []
    for i in range(2 * NC):
        rows = rows_of((hisrow if i < NC else myrow) + (i % NC) * CHUNK, CHUNK)
        both = (
            pltpu.make_async_copy(g_hbm.at[:, rows], g_in.at[:, rows], ld_g.at[i]),
            pltpu.make_async_copy(e_hbm.at[:, rows], e_in.at[:, rows], ld_e.at[i]),
        )
        for c in both:
            c.start()
        loads.append(both)

    load_q.wait()
    qh, ql = pair(q_in[...])
    q_left = jnp.concatenate(
        [jnp.concatenate([qh, qh], axis=1), jnp.concatenate([ql, ql], axis=1)], axis=0
    )

    def partial(i):
        for c in loads[i]:
            c.wait()
        first = (hisrow if i < NC else myrow) + (i % NC) * CHUNK
        rows = rows_of(first, CHUNK)
        for g in range(GROUPS):
            total = g_in[g, rows].astype(F32) + e_in[g, rows]
            merged[g, rows] = total
            out = dot(q_left, jnp.concatenate(pair(total), axis=1), NT)
            out = out[:RANK] + out[RANK:]
            for b in range(CHUNK // COLS):
                part[rows_of(first + b * COLS + g * RANK, RANK)] = out[:, b * COLS : (b + 1) * COLS]

    def to_sibling(i):
        return remote(part.at[rows_of(hisrow + i * CHUNK, CHUNK)], sib.at[pl.ds(i * CHUNK, CHUNK)],
                      sib_s.at[i], sib_r.at[i], sibling)

    def m_to_sibling(g):
        return remote(merged.at[g, rows_of(myrow, HALF)], m_sib.at[g], m_s, m_r, sibling)

    for i in range(NC):
        partial(i)
        if i == 0:
            pl.semaphore_wait(barrier, len(greeted))
        to_sibling(i).start()
    for i in range(NC):
        partial(NC + i)
    for g in range(GROUPS):
        m_to_sibling(g).start()
    for i in range(NC):
        to_sibling(i).wait_recv()
        at = pl.ds(i * CHUNK, CHUNK)
        summed[at] = part[rows_of(myrow + i * CHUNK, CHUNK)] + sib[at]

    streams = []
    base = 0
    for n, (axes, size) in enumerate(STREAMS):
        streams.append((axes, size, base, *per_stream[10 * n : 10 * n + 10]))
        base += MEMBERS[axes] * size
    assert base == HALF

    def count(stream, step):
        return MEMBERS[OTHER[stream[0]] if step == 2 else stream[0]]

    def scatter(stream, j):
        axes, size, base, inbox, _, _, _, s1, r1, *_ = stream
        to = member(axes, offsets[axes][j])
        return remote(summed.at[rows_of(base + to * size, size)], inbox.at[j], s1, r1, device(axes, to))

    def exchange(stream, j):
        axes, size, base, _, box, mid, _, _, _, s2, r2, _, _ = stream
        axes = OTHER[axes]
        return remote(mid, box.at[place[axes]], s2, r2, device(axes, member(axes, offsets[axes][j])))

    def gather(stream, j):
        axes, size, base, _, _, _, done, *_, s3, r3 = stream
        target = p_all.at[rows_of(myrow + base + place[axes] * size, size)]
        return remote(done, target, s3, r3, device(axes, member(axes, offsets[axes][j])))

    def whole(stream, step):
        axes, size, base, inbox, box, _, _, s1, r1, s2, r2, s3, r3 = stream
        what = inbox if step == 1 else box if step == 2 else p_all.at[pl.ds(0, count(stream, 3) * size)]
        send, recv = ((s1, r1), (s2, r2), (s3, r3))[step - 1]
        return remote(what, what, send, recv, sibling)

    for j in range(X * Y):
        for stream in streams:
            if j < count(stream, 1):
                scatter(stream, j).start()

    for stream in streams:
        axes, size, base, inbox, box, mid, *_ = stream
        whole(stream, 1).wait_recv()
        total = inbox[0]
        for j in range(1, count(stream, 1)):
            total = total + inbox[j]
        mid[...] = total
        for j in range(count(stream, 2)):
            exchange(stream, j).start()

    all_m = remote(m_sib, m_sib, m_s, m_r, sibling)
    all_m.wait_recv()

    def chip_pairs(i, _):
        at = pl.ds(pl.multiple_of(i * UNIT, UNIT), UNIT)
        for g in range(GROUPS):
            hi, lo = pair(merged[g, rows_of(hisrow + i * UNIT, UNIT)] + m_sib[g, at])
            s_pair[g, at] = jnp.concatenate([hi, lo], axis=1)
        return 0

    lax.fori_loop(0, HALF // UNIT, chip_pairs, 0)

    for stream in streams:
        axes, size, base, inbox, box, mid, done, *_ = stream
        whole(stream, 2).wait_recv()
        total = box[0]
        for j in range(1, count(stream, 2)):
            total = total + box[j]
        done[...] = total
        for j in range(count(stream, 3)):
            gather(stream, j).start()

    for stream in streams:
        whole(stream, 3).wait_recv()

    def forward(base):
        half = p_all.at[rows_of(base, HALF)]
        return remote(half, half, fw_s, fw_r, sibling)

    def turned(base):
        blocks = [p_all[rows_of(base + b * COLS, COLS)] for b in range(HALF // COLS)]
        return blocks, pair(jnp.concatenate(blocks, axis=1))

    def store_rows(base, blocks):
        for b, block in enumerate(blocks):
            p_pair[rows_of(base + b * COLS, COLS)] = jnp.concatenate(pair(block.T), axis=1)

    blocks, halves = turned(hisrow)
    left = [
        jnp.concatenate([v[g * RANK : (g + 1) * RANK] for g in range(GROUPS)], axis=1) for v in halves
    ]
    acc = dot(jnp.concatenate(left, axis=0), s_pair[...].reshape(GROUPS * HALF, 2 * COLS))
    t_mine[...] = quarters(acc, RANK, COLS)

    up = remote(t_mine, t_sib, tu_s, tu_r, sibling)

    @pl.when(core == 0)
    def _():
        up.start()

    both = jnp.concatenate(halves, axis=0)
    gram = quarters(dot(both, both, NT), COLS, COLS)
    small = gram[:RANK, :RANK]
    for g in range(1, GROUPS):
        small = small + gram[g * RANK : (g + 1) * RANK, g * RANK : (g + 1) * RANK]
    g_mine[...] = small
    swap = remote(g_mine, g_sib, g_s, g_r, sibling)
    swap.start()
    forward(hisrow).start()

    others = from_zt.at[pl.ds(0, Z - 1)]
    all_terms = remote(others, others, tz_s, tz_r, sibling)

    @pl.when(core == 1)
    def _():
        up.wait_recv()
        from_zt[z] = t_mine[...] + t_sib[...]
        for o in LINE[:-1]:
            remote(from_zt.at[z], from_zt.at[z], tz_s, tz_r, (member("z", o) * 2 + 1, me)).start()

    store_rows(hisrow, blocks)
    swap.wait()
    linv = inverse_factor(g_mine[...] + g_sib[...])
    linv_ref[...] = linv
    ginv_ref[...] = dot(linv, linv, TN, lax.Precision.HIGHEST)
    forward(myrow).wait_recv()
    store_rows(myrow, turned(myrow)[0])

    for i in range(NC):
        to_sibling(i).wait_send()
    all_m.wait_send()
    for stream in streams:
        for step in (1, 2, 3):
            whole(stream, step).wait_send()
    forward(hisrow).wait_send()

    down = remote(t_all, t_all, td_s, td_r, sibling)

    @pl.when(core == 1)
    def _():
        all_terms.wait_recv()
        total = from_zt[0]
        for k in range(1, Z):
            total = total + from_zt[k]
        t_all[...] = total
        down.start()
        all_terms.wait_send()
        down.wait_send()

    @pl.when(core == 0)
    def _():
        up.wait_send()
        down.wait_recv()

    terms_ref[...] = t_all[...]


def share(q_t, grads, error):
    sems = pltpu.SemaphoreType.DMA
    hbm = pl.BlockSpec(memory_space=pltpu.HBM)
    args = (q_t, grads.reshape(GROUPS, ROWS, COLS), error.reshape(GROUPS, ROWS, COLS))
    per_stream = []
    for axes, size in STREAMS:
        first, second = MEMBERS[axes], MEMBERS[OTHER[axes]]
        per_stream += [
            pltpu.VMEM((first, size, COLS), F32),
            pltpu.VMEM((second, size, COLS), F32),
            pltpu.VMEM((size, COLS), F32),
            pltpu.VMEM((size, COLS), F32),
            sems, sems, sems, sems, sems, sems,
        ]
    return pl.pallas_call(
        share_kernel,
        name="share",
        out_shape=(
            pltpu.VMEM((GROUPS, ROWS, COLS), F32),
            pltpu.VMEM((ROWS, 2 * COLS), BF16),
            pltpu.VMEM((RANK, RANK), F32),
            pltpu.VMEM((RANK, RANK), F32),
            pltpu.VMEM((RANK, COLS), F32),
        ),
        in_specs=[hbm] * 3,
        out_specs=[pl.BlockSpec(memory_space=pltpu.VMEM)] * 5,
        scratch_shapes=[
            pltpu.VMEM((RANK, COLS), F32),
            pltpu.VMEM((GROUPS, ROWS, COLS), BF16),
            pltpu.VMEM((GROUPS, ROWS, COLS), F32),
            pltpu.VMEM((ROWS, COLS), F32),
            pltpu.VMEM((HALF, COLS), F32),
            pltpu.VMEM((HALF, COLS), F32),
            pltpu.VMEM((ROWS, COLS), F32),
            pltpu.VMEM((GROUPS, HALF, COLS), F32),
            pltpu.VMEM((GROUPS, HALF, 2 * COLS), BF16),
            pltpu.VMEM((Z, RANK, COLS), F32),
            pltpu.VMEM((RANK, COLS), F32),
            pltpu.VMEM((RANK, COLS), F32),
            pltpu.VMEM((RANK, COLS), F32),
            pltpu.VMEM((RANK, RANK), F32),
            pltpu.VMEM((RANK, RANK), F32),
            sems, sems((2 * NC,)), sems((2 * NC,)),
            sems((NC,)), sems((NC,)), sems, sems, sems, sems,
            sems, sems, sems, sems, sems, sems, sems, sems,
            *per_stream,
        ],
        compiler_params=pltpu.CompilerParams(
            collective_id=0, has_side_effects=True, vmem_limit_bytes=32 * 1024 * 1024
        ),
    )(*(pltpu.with_memory_space_constraint(a, pltpu.HBM) for a in args))


def finish_kernel(
    replicas, merged, p_pair, linv_ref, ginv_ref, terms_ref, synced, error_out, q_ref, right, out, rows_out, sem, sem_rows
):
    dp = lax.axis_index("dp")
    highest = lax.Precision.HIGHEST
    right[...] = jnp.zeros_like(right)
    terms = terms_ref[...] / replicas
    hi, lo = pair(dot(ginv_ref[...], terms, precision=highest))
    both = jnp.concatenate([hi, lo], axis=1)
    for g in range(GROUPS):
        right[g, pl.ds(g * RANK, RANK)] = both
        right[g, pl.ds(COLS + g * RANK, RANK)] = both

    def approx(g, rows):
        wide = dot(p_pair[rows], right[g])
        return wide[:, :COLS] + wide[:, COLS:]

    copies = []
    units = [(g, i * UNIT) for i in range(ROWS // UNIT) for g in range(GROUPS)]
    for n, (g, first) in enumerate(units):
        rows = pl.ds(first, UNIT)
        out[g, rows] = merged[g, rows] - approx(g, rows)
        copies.append(pltpu.make_async_copy(out.at[g, rows], error_out.at[g, rows], sem.at[n]))
        copies[-1].start()
        if n == len(units) // 2:
            own = D // replicas
            per = ROWS // own
            rows = pl.ds(pl.multiple_of(lax.rem(dp, per) * own, own), own)
            rows_out[...] = approx(lax.div(dp, per), rows).astype(BF16)
            copies.append(pltpu.make_async_copy(rows_out, synced, sem_rows))
            copies[-1].start()
    q_ref[...] = dot(linv_ref[...], terms, precision=highest)
    for c in copies:
        c.wait()


def finish(replicas, *operands):
    def body(*refs):
        finish_kernel(replicas, *refs)

    sems = pltpu.SemaphoreType.DMA
    own = D // replicas
    vmem, hbm = pl.BlockSpec(memory_space=pltpu.VMEM), pl.BlockSpec(memory_space=pl.ANY)
    return pl.pallas_call(
        body,
        name="finish",
        out_shape=(
            jax.ShapeDtypeStruct((own, COLS), BF16),
            jax.ShapeDtypeStruct((GROUPS, ROWS, COLS), F32),
            jax.ShapeDtypeStruct((RANK, COLS), F32),
        ),
        in_specs=[vmem] * 5,
        out_specs=[hbm, hbm, vmem],
        scratch_shapes=[
            pltpu.VMEM((GROUPS, 2 * COLS, 2 * COLS), BF16),
            pltpu.VMEM((GROUPS, ROWS, COLS), F32),
            pltpu.VMEM((own, COLS), BF16),
            sems((D // UNIT,)),
            sems,
        ],
        compiler_params=pltpu.CompilerParams(vmem_limit_bytes=16 * 1024 * 1024),
    )(*(pltpu.with_memory_space_constraint(a, pltpu.VMEM) for a in operands))


def solution(mesh):
    replicas = mesh.shape["dp"]

    def on_device(grads, error, q_prev):
        synced, error_out, q_t = finish(replicas, *share(q_prev.T, grads, error))
        return synced, error_out.reshape(1, D, COLS), q_t.T

    placed = (P("dp", None, "tensor"), P("dp", None, "tensor"), P("tensor", None))
    return jax.shard_map(
        on_device,
        mesh=mesh,
        in_specs=placed,
        out_specs=(P("dp", "tensor"), P("dp", None, "tensor"), P("tensor", None)),
        check_vma=False,
    )
```
